256 devices in a mesh: wide: 32 (over x, y, core), narrow: 8 (over z).
Axes of the slice: x: 4, y: 4, z: 8, core: 2. Of those that a mesh axis runs over, the one named last changes fastest.
Arguments:
- saved_codes: bfloat16 [768, 8192], P('wide', 'narrow'), may hold values from -4 to 4
- saved_scale: float32 [32, 8], P('wide', 'narrow'), may hold values from 0.5 to 2
- grad_output: bfloat16 [768, 8192], P('wide', 'narrow'), may hold values from -45 to 45
- gate_codes: bfloat16 [8192, 28672], P('narrow', 'wide'), may hold values from -0.0625 to 0.0625
- gate_scale: float32 [8, 32], P('narrow', 'wide'), may hold values from 0.5 to 2
- up_codes: bfloat16 [8192, 28672], P('narrow', 'wide'), may hold values from -0.0625 to 0.0625
- up_scale: float32 [8, 32], P('narrow', 'wide'), may hold values from 0.5 to 2
- down_codes: bfloat16 [28672, 8192], P('wide', 'narrow'), may hold values from -0.03125 to 0.03125
- down_scale: float32 [32, 8], P('wide', 'narrow'), may hold values from 0.5 to 2
Outputs:
- gate_out: bfloat16 [8192, 28672], P('narrow', 'wide')
- up_out: bfloat16 [8192, 28672], P('narrow', 'wide')
- down_out: bfloat16 [28672, 8192], P('wide', 'narrow')
- input_out: bfloat16 [768, 8192], P('wide', 'narrow')
- amaxes: float32 [4], replicated
The draws below stay inside these ranges and needn't reach their ends.
All inputs are finite; a program needn't handle non-finite values. Where the reference program divides by a largest or mean magnitude, that divisor is 1e-20 or more.
Results may differ from the reference program's by a relative error of at most 0.0079.
Values may be sent and summed in bfloat16 or wider, within the bound.
A program may use at most 128 MiB of HBM per device.

```python
import math
import jax
import jax.numpy as jnp

D = 8192
FF = 28672
TOK_DEV = 24
TOKENS = 768
N_WIDE = 32
N_NARROW = 8


def draw_grad_output(key, part):
    key = jax.random.fold_in(key, 11)
    first, second, third = jax.random.split(key, 3)
    position = jnp.arange(TOKENS, dtype=jnp.float32)[:, None] / TOKENS
    base = jnp.clip(jax.random.normal(first, (TOKENS, D), jnp.float32), -4.0, 4.0)
    spread = math.log(3.0)
    row_factor = jnp.exp(math.log(3.0) * position + jax.random.uniform(second, (TOKENS, 1), jnp.float32, 0.0, spread))
    col_factor = jnp.exp(jax.random.uniform(third, (1, D), jnp.float32, 0.0, math.log(3.5)))
    return (0.3 * base * row_factor * col_factor).astype(jnp.bfloat16)


def levels(own_key, shape, cuts, smallest, high):
    loudness, own = 1.0, jax.random.fold_in(own_key, 6)
    for dim, blocks in cuts:
        steps = jnp.exp(jax.random.uniform(jax.random.fold_in(own, dim), (blocks,), jnp.float32, smallest / len(cuts), high / len(cuts)))
        loudness = loudness * jnp.repeat(steps, shape[dim] // blocks).reshape([-1 if axis == dim else 1 for axis in range(len(shape))])
    return loudness


def gaussian(own_key, dims, deviation, limit, shards=(), held_as=jnp.bfloat16):
    result = jax.random.normal(own_key, dims, jnp.float32) * deviation
    if len(shards) > 0:
        result = levels(own_key, dims, shards, -0.22, 0.18) * result
    return jnp.clip(result, min=-limit, max=limit).astype(held_as)


def setup_inputs(seed: int = 0) -> dict:
    keys = jax.random.split(jax.random.key(seed), 10)
    saved_codes = gaussian(keys[0], (TOKENS, D), 1.0, 4.0, ((0, 32), (1, 8)))
    saved_scale = jnp.clip(jnp.exp(math.log(2.0) - 1.3862944 * jax.random.uniform(keys[1], (N_WIDE, N_NARROW), jnp.float32) ** levels(keys[1], (N_WIDE, N_NARROW), ((0, 32), (1, 8)), -0.2, 0.2)), 0.5, 2.0)
    grad_output = draw_grad_output(jax.random.fold_in(keys[9], 71), 0)
    gate_codes = gaussian(keys[3], (D, FF), D ** -0.5, 0.0625, ((0, 8), (1, 32)))
    gate_scale = jnp.clip(jnp.exp(math.log(2.0) - 1.3862944 * jax.random.uniform(keys[4], (N_NARROW, N_WIDE), jnp.float32) ** levels(keys[4], (N_NARROW, N_WIDE), ((0, 8), (1, 32)), -0.2, 0.2)), 0.5, 2.0)
    up_codes = gaussian(keys[5], (D, FF), D ** -0.5, 0.0625, ((0, 8), (1, 32)))
    up_scale = jnp.clip(jnp.exp(math.log(2.0) - 1.3862944 * jax.random.uniform(keys[6], (N_NARROW, N_WIDE), jnp.float32) ** levels(keys[6], (N_NARROW, N_WIDE), ((0, 8), (1, 32)), -0.2, 0.2)), 0.5, 2.0)
    down_codes = gaussian(keys[7], (FF, D), FF ** -0.5, 0.03125, ((0, 32), (1, 8)))
    down_scale = jnp.clip(jnp.exp(math.log(2.0) - 1.3862944 * jax.random.uniform(keys[8], (N_WIDE, N_NARROW), jnp.float32) ** levels(keys[8], (N_WIDE, N_NARROW), ((0, 32), (1, 8)), -0.2, 0.2)), 0.5, 2.0)
    return dict(saved_codes=saved_codes, saved_scale=saved_scale, grad_output=grad_output, gate_codes=gate_codes, gate_scale=gate_scale, up_codes=up_codes, up_scale=up_scale, down_codes=down_codes, down_scale=down_scale)


eps = 1e-6


def block_product(operand, codes_mat, scales):
    blocks = scales.shape[0]
    span_rows = operand.shape[1] // blocks
    span_cols = codes_mat.shape[1] // scales.shape[1]
    summed = jnp.zeros((operand.shape[0], codes_mat.shape[1]), jnp.float32)
    for which_block in range(blocks):
        lower = which_block * span_rows
        upper = lower + span_rows
        partial_sum = jnp.dot(operand[:, lower:upper], codes_mat[lower:upper], preferred_element_type=jnp.float32)
        summed = summed + partial_sum * jnp.repeat(scales[which_block], span_cols)[None, :]
    return summed


def unit_grads(gate_pre, up_pre, hidden_grad):
    sigmoid_gate = jax.nn.sigmoid(gate_pre)
    silu_gate = gate_pre * sigmoid_gate
    hidden = (silu_gate * up_pre).astype(jnp.bfloat16)
    gate_grad = (hidden_grad * up_pre * sigmoid_gate * (1.0 + gate_pre * (1.0 - sigmoid_gate))).astype(jnp.bfloat16)
    up_grad = (hidden_grad * silu_gate).astype(jnp.bfloat16)
    return hidden, gate_grad, up_grad


def encode(gradient):
    largest = jnp.max(jnp.abs(gradient)) + eps
    return (gradient / largest).astype(jnp.bfloat16), largest


def reference(saved_codes, saved_scale, grad_output, gate_codes, gate_scale, up_codes, up_scale, down_codes, down_scale):
    full_scale = jnp.repeat(jnp.repeat(saved_scale, TOK_DEV, 0), D // N_NARROW, 1)
    saved = (saved_codes.astype(jnp.float32) * full_scale).astype(jnp.bfloat16)
    gate_pre = block_product(saved, gate_codes, gate_scale)
    up_pre = block_product(saved, up_codes, up_scale)
    hidden_grad = block_product(grad_output, down_codes.T, down_scale.T)
    hidden, gate_grad, up_grad = unit_grads(gate_pre, up_pre, hidden_grad)
    down_out, down_amax = encode(jnp.dot(hidden.T, grad_output, preferred_element_type=jnp.float32))
    gate_out, gate_amax = encode(jnp.dot(saved.T, gate_grad, preferred_element_type=jnp.float32))
    up_out, up_amax = encode(jnp.dot(saved.T, up_grad, preferred_element_type=jnp.float32))
    input_grad = block_product(gate_grad, gate_codes.T, gate_scale.T) + block_product(up_grad, up_codes.T, up_scale.T)
    input_out, input_amax = encode(input_grad)
    amaxes = jnp.stack([gate_amax, up_amax, down_amax, input_amax]).astype(jnp.float32)
    return gate_out, up_out, down_out, input_out, amaxes
```

```python
import jax
import jax.numpy as jnp
from jax import lax
from jax.experimental import pallas as pl
from jax.experimental.pallas import tpu as pltpu
from jax.sharding import PartitionSpec as P

eps = 1e-06
F32 = jnp.float32
BF16 = jnp.bfloat16
TOK, FEAT, UNIT = 768, 1024, 896
HALF = FEAT // 2
BLK = 48
CH = 96
NSEM = 200


def mm(lhs, rhs):
    return jnp.dot(lhs, rhs, preferred_element_type=F32)


def mm_last(lhs, rhs):
    return lax.dot_general(lhs, rhs, (((1,), (1,)), ((), ())), preferred_element_type=F32)


def mm_first(lhs, rhs):
    return lax.dot_general(lhs, rhs, (((0,), (0,)), ((), ())), preferred_element_type=F32)


def largest(value):
    rows, cols = value.shape
    folded = jnp.max(jnp.abs(value).reshape(rows // 8, 8, cols), axis=0)
    result = folded[:, :128]
    for start in range(128, cols, 128):
        result = jnp.maximum(result, folded[:, start : start + 128])
    return result


def kernel(
    saved_scale,
    gate_scale,
    up_scale,
    down_scale,
    saved_codes,
    grad_output,
    gate_hbm,
    up_hbm,
    down_hbm,
    gate_w,
    up_w,
    down_w,
    input_o,
    amax_o,
    X,
    W,
    DN,
    E,
    SE,
    RB,
    SB,
    H,
    PRE,
    IGK,
    IGS,
    CR,
    CS,
    RA,
    BS,
    RBB,
    FS,
    FIN,
    FX,
    MX,
    MR,
    send_sem,
    recv_sem,
    load_sem,
):
    wide = lax.axis_index("wide")
    z = lax.axis_index("narrow")
    core = lax.rem(wide, 2)
    x = wide // 8
    y = lax.rem(wide // 2, 4)
    a = x + core * (y - x)
    b = y + core * (x - y)

    def at(da, db):
        pa = lax.rem(a + da + 4, 4)
        pb = lax.rem(b + db + 4, 4)
        return pa + core * (pb - pa), pb + core * (pa - pb)

    def dev(da, db):
        px, py = at(da, db)
        return (px * 8 + py * 2 + core, z)

    def off(da, db):
        px, py = at(da, db)
        rel = lax.rem(px * 2 + py // 2 - z + 8, 8)
        far = rel // 4
        base = (1 - far) * (672 - 192 * rel) + far * 192 * (rel - 4)
        return pl.multiple_of(base + lax.rem(py, 2) * BLK, 16)

    partner = (wide + 1 - 2 * core, z)
    right = (wide, lax.rem(z + 1, 8))
    left = (wide, lax.rem(z + 7, 8))

    loads = []
    for arr, src in ((0, gate_hbm), (1, up_hbm)):
        for half in range(2):
            loads.append(
                pltpu.make_async_copy(
                    src.at[pl.ds(half * HALF, HALF)], W.at[arr, half], load_sem.at[len(loads)]
                )
            )
    loads.append(pltpu.make_async_copy(down_hbm, DN, load_sem.at[4]))
    for load in loads:
        load.start()

    barrier = pltpu.get_barrier_semaphore()
    others = [partner]
    others += [(wide, lax.rem(z + k, 8)) for k in range(1, 8)]
    others += [dev(k, 0) for k in range(1, 4)] + [dev(0, k) for k in range(1, 4)]
    for other in others:
        pl.semaphore_signal(barrier, inc=1, device_id=other, device_id_type=pl.DeviceIdType.MESH)

    started = []

    def send(src, dst, device):
        k = len(started)
        copy = pltpu.make_async_remote_copy(
            src_ref=src,
            dst_ref=dst,
            send_sem=send_sem.at[k],
            recv_sem=recv_sem.at[k],
            device_id=device,
            device_id_type=pl.DeviceIdType.MESH,
        )
        copy.start()
        started.append(copy)
        return copy

    first_core = core == 0
    tokens = [saved_codes[...].astype(F32) * saved_scale[0, 0], grad_output[...].astype(F32)]
    for t in range(2):
        low, high = tokens[t][:, :HALF], tokens[t][:, HALF:]
        E[t, core] = jnp.where(first_core, low, high)
        SE[t] = jnp.where(first_core, high, low)
    pl.semaphore_wait(barrier, len(others))
    swaps = [send(SE.at[t], E.at[t, core], partner) for t in range(2)]

    def gather(t):
        def full(da, db, device):
            ref = X.at[t, core, pl.ds(off(da, db), BLK)]
            return send(ref, ref, device)

        def part(da, db, q, device):
            ref = X.at[t, core, pl.ds(off(da, db), BLK), pl.ds(q * (HALF // 2), HALF // 2)]
            return send(ref, ref, device)

        swaps[t].wait_recv()
        X[t, core, pl.ds(off(0, 0), BLK)] = jnp.concatenate([E[t, 0], E[t, 1]], axis=0).astype(BF16)
        to_ap, to_am = full(0, 0, dev(1, 0)), full(0, 0, dev(-1, 0))
        bp, bm = [full(0, 0, dev(0, 1))], [full(0, 0, dev(0, -1))]
        pairs = [full(0, 0, partner)]
        yield
        order = [0, -1, 1, 2]
        to_ap.wait_recv()
        half_p = part(-1, 0, 0, dev(1, 0))
        bp.append(full(-1, 0, dev(0, 1)))
        bm.append(full(-1, 0, dev(0, -1)))
        pairs.append(full(-1, 0, partner))
        to_am.wait_recv()
        half_m = part(1, 0, 1, dev(-1, 0))
        bp.append(full(1, 0, dev(0, 1)))
        bm.append(full(1, 0, dev(0, -1)))
        pairs.append(full(1, 0, partner))
        yield
        half_p.wait_recv()
        half_m.wait_recv()
        bp.append(full(2, 0, dev(0, 1)))
        bm.append(full(2, 0, dev(0, -1)))
        pairs.append(full(2, 0, partner))
        yield
        hp, hm = [], []
        for i in range(4):
            bp[i].wait_recv()
            hp.append(part(order[i], -1, 0, dev(0, 1)))
            pairs.append(full(order[i], -1, partner))
            bm[i].wait_recv()
            hm.append(part(order[i], 1, 1, dev(0, -1)))
            pairs.append(full(order[i], 1, partner))
            if i % 2 == 1:
                yield
        for i in range(4):
            hp[i].wait_recv()
            hm[i].wait_recv()
            pairs.append(full(order[i], 2, partner))
        yield
        for pair in pairs:
            pair.wait_recv()

    def run(gen):
        for _ in gen:
            pass

    def step(gen):
        next(gen, None)

    run(gather(0))
    grads = gather(1)
    step(grads)

    scales = [gate_scale[0, 0], up_scale[0, 0], down_scale[0, 0]]

    def partial(arr, start, count):
        rows = pl.ds(start, count)
        if arr < 2:
            value = mm(X[0, 0, rows], W[arr, 0]) + mm(X[0, 1, rows], W[arr, 1])
        else:
            value = mm_last(X[1, 0, rows], DN[:, :HALF]) + mm_last(X[1, 1, rows], DN[:, HALF:])
        return value * scales[arr]

    def reduce(arr):
        def to_right(src, dst, count=CH):
            return send(SB.at[arr, pl.ds(src, count)], RB.at[arr, pl.ds(dst, count)], right)

        def to_left(src, dst, count=CH):
            return send(SB.at[arr, pl.ds(src, count)], RB.at[arr, pl.ds(dst, count)], left)

        SB[arr, 0:96] = partial(arr, 0, 96).astype(BF16)
        flow = [to_right(0, 96, BLK), to_left(48, 240, BLK)]
        yield
        value = partial(arr, 96, 192)
        SB[arr, 144:240] = value[48:144].astype(BF16)
        flow[0].wait_recv()
        SB[arr, 96:144] = (value[0:48] + RB[arr, 96:144].astype(F32)).astype(BF16)
        right_flow = to_right(96, 288)
        flow[1].wait_recv()
        SB[arr, 240:288] = (value[144:192] + RB[arr, 240:288].astype(F32)).astype(BF16)
        flow = [right_flow, to_left(192, 384)]
        yield
        for start in (288, 480):
            value = partial(arr, start, 192)
            flow[0].wait_recv()
            SB[arr, start : start + 96] = (value[:96] + RB[arr, start : start + 96].astype(F32)).astype(BF16)
            right_flow = to_right(start, start + 192)
            flow[1].wait_recv()
            SB[arr, start + 96 : start + 192] = (
                value[96:] + RB[arr, start + 96 : start + 192].astype(F32)
            ).astype(BF16)
            flow = [right_flow, to_left(start + 96, start + 288)]
            yield
        value = partial(arr, 672, 96)
        flow[0].wait_recv()
        flow[1].wait_recv()
        PRE[arr] = value + RB[arr, 672:768].astype(F32) + RB[arr, 768:864].astype(F32)
        yield

    def spread(arr):
        def to_right(src, dst, count=CH):
            return send(H.at[arr, pl.ds(src, count)], H.at[arr, pl.ds(dst, count)], right)

        def to_left(src, dst, count=CH):
            return send(H.at[arr, pl.ds(src, count)], H.at[arr, pl.ds(dst, count)], left)

        flow = [to_right(672, 576), to_left(672, 480)]
        yield
        flow[0].wait_recv()
        right_flow = to_right(576, 384)
        flow[1].wait_recv()
        flow = [right_flow, to_left(480, 288)]
        yield
        flow[0].wait_recv()
        right_flow = to_right(384, 192)
        flow[1].wait_recv()
        flow = [right_flow, to_left(288, 96)]
        yield
        flow[0].wait_recv()
        right_flow = to_right(192, 0, BLK)
        flow[1].wait_recv()
        flow = [right_flow, to_left(144, 48, BLK)]
        yield
        flow[0].wait_recv()
        flow[1].wait_recv()
        yield

    for load in loads[:4]:
        load.wait()
    gate_sum, up_sum, hidden_sum = reduce(0), reduce(1), reduce(2)
    for _ in range(3):
        step(gate_sum)
        step(grads)
        step(up_sum)
        step(grads)
    step(gate_sum)
    step(grads)
    step(up_sum)
    run(grads)
    loads[4].wait()
    step(hidden_sum)
    step(gate_sum)
    step(up_sum)

    def hidden_rows(i, carry):
        rows = pl.ds(pl.multiple_of(i * 16, 16), 16)
        gate_pre = PRE[0, rows]
        H[0, pl.ds(pl.multiple_of(672 + i * 16, 16), 16)] = (
            gate_pre * jax.nn.sigmoid(gate_pre) * PRE[1, rows]
        ).astype(BF16)
        return carry

    lax.fori_loop(0, 6, hidden_rows, 0)
    hidden_all, gate_all, up_all = spread(0), spread(1), spread(2)
    step(hidden_all)
    for _ in range(4):
        step(hidden_sum)

    def grad_rows(i, carry):
        rows = pl.ds(pl.multiple_of(i * 16, 16), 16)
        out = pl.ds(pl.multiple_of(672 + i * 16, 16), 16)
        gate_pre = PRE[0, rows]
        hidden_grad = PRE[2, rows]
        sig = jax.nn.sigmoid(gate_pre)
        H[1, out] = (hidden_grad * PRE[1, rows] * sig * (1.0 + gate_pre * (1.0 - sig))).astype(BF16)
        H[2, out] = (hidden_grad * gate_pre * sig).astype(BF16)
        return carry

    lax.fori_loop(0, 6, grad_rows, 0)
    step(gate_all)
    step(up_all)

    def weight_part(kind, start, count, first, last):
        def tile(i, top):
            rows = pl.ds(start, count)
            if kind < 2:
                ref = (gate_w, up_w)[kind]
                half = i // 2
                cols = pl.ds(pl.multiple_of(lax.rem(i, 2) * 256, 256), 256)
                value = mm_first(X[0, half, rows, cols], H[1 + kind, rows])
                where = pl.ds(pl.multiple_of(i * 256, 256), 256)
                if not first:
                    value = value + ref[where]
                ref[where] = value
            else:
                cols = pl.ds(pl.multiple_of(i * 128, 128), 128)
                value = jnp.concatenate(
                    [mm_first(H[0, rows, cols], X[1, half, rows]) for half in range(2)], axis=1
                )
                if not first:
                    value = value + down_w[cols]
                down_w[cols] = value
            return jnp.maximum(top, largest(value)) if last else top

        top = lax.fori_loop(0, 4 if kind < 2 else 7, tile, jnp.zeros((8, 128), F32))
        if last:
            MX[0, kind] = top

    pulls = []

    def input_part(start, count):
        rows = pl.ds(start, count)

        def half_value(half):
            return scales[0] * mm_last(H[1, rows], W[0, half]) + scales[1] * mm_last(H[2, rows], W[1, half])

        IGS[rows] = half_value(1 - core).astype(BF16)
        pulls.append(send(IGS.at[rows], CR.at[rows], partner))
        IGK[rows] = half_value(core)

    step(gate_all)
    step(up_all)
    input_part(480, 288)
    step(gate_all)
    step(up_all)
    input_part(288, 192)
    weight_part(0, 288, 480, True, False)
    step(gate_all)
    step(up_all)
    step(hidden_all)
    weight_part(1, 288, 480, True, False)
    input_part(96, 192)
    step(gate_all)
    step(up_all)
    input_part(0, 96)
    step(hidden_all)

    for pull in pulls:
        pull.wait_recv()
    across = []
    for da in range(1, 4):
        for db in range(4):
            rows = pl.ds(off(da, db), BLK)
            CS[da - 1, db] = (IGK[rows] + CR[rows].astype(F32)).astype(BF16)
        across.append(send(CS.at[da - 1], RA.at[da - 1], dev(da, 0)))
    weight_part(0, 96, 192, False, False)
    weight_part(1, 96, 192, False, False)
    step(hidden_all)
    weight_part(0, 0, 96, False, True)
    for copy in across:
        copy.wait_recv()
    along = []
    for db in (1, 2, 3, 0):
        rows = pl.ds(off(0, db), BLK)
        value = IGK[rows] + CR[rows].astype(F32)
        for k in range(3):
            value = value + RA[k, db].astype(F32)
        if db == 0:
            FS[...] = value
        else:
            BS[db - 1] = value.astype(BF16)
            along.append(send(BS.at[db - 1], RBB.at[db - 1], dev(0, db)))
    weight_part(1, 0, 96, False, True)
    weight_part(2, 288, 480, True, False)
    for copy in along:
        copy.wait_recv()
    value = FS[...]
    for k in range(3):
        value = value + RBB[k].astype(F32)
    FIN[0] = value[:24]
    FIN[1] = value[24:]
    last = send(FIN.at[1 - core], FX, partner)
    step(hidden_all)
    weight_part(2, 0, 288, False, True)
    last.wait_recv()
    mine, theirs = FIN[core], FX[...]
    low = jnp.where(first_core, mine, theirs)
    high = jnp.where(first_core, theirs, mine)
    input_o[:, :HALF] = low
    input_o[:, HALF:] = high
    MX[0, 3] = jnp.maximum(largest(low), largest(high))

    base = 0
    groups = [
        [(wide, lax.rem(z + k, 8)) for k in range(1, 8)],
        [dev(k, 0) for k in range(1, 4)],
        [dev(0, k) for k in range(1, 4)],
        [partner],
    ]
    for phase, group in enumerate(groups):
        copies = [send(MX.at[phase], MR.at[base + k], other) for k, other in enumerate(group)]
        value = MX[phase]
        for k, copy in enumerate(copies):
            copy.wait_recv()
            value = jnp.maximum(value, MR[base + k])
        MX[phase + 1] = value
        base += len(group)
    for k in range(4):
        amax_o[k : k + 1] = jnp.full((1, 128), jnp.max(MX[4, k]) + eps, F32)
    amax_o[4:] = jnp.zeros((4, 128), F32)

    for copy in started:
        copy.wait_send()


def per_device(
    saved_codes,
    saved_scale,
    grad_output,
    gate_codes,
    gate_scale,
    up_codes,
    up_scale,
    down_codes,
    down_scale,
):
    smem = pl.BlockSpec(memory_space=pltpu.SMEM)
    vmem = pl.BlockSpec(memory_space=pltpu.VMEM)
    hbm = pl.BlockSpec(memory_space=pl.ANY)
    gate_w, up_w, down_w, input_w, tops = pl.pallas_call(
        kernel,
        out_shape=[
            pltpu.VMEM((FEAT, UNIT), F32),
            pltpu.VMEM((FEAT, UNIT), F32),
            pltpu.VMEM((UNIT, FEAT), F32),
            pltpu.VMEM((24, FEAT), F32),
            pltpu.VMEM((8, 128), F32),
        ],
        in_specs=[smem] * 4 + [vmem] * 2 + [hbm] * 3,
        out_specs=[vmem] * 5,
        scratch_shapes=[
            pltpu.VMEM((2, 2, TOK, HALF), BF16),
            pltpu.VMEM((2, 2, HALF, UNIT), BF16),
            pltpu.VMEM((UNIT, FEAT), BF16),
            pltpu.VMEM((2, 2, 24, HALF), F32),
            pltpu.VMEM((2, 24, HALF), F32),
            pltpu.VMEM((3, 864, UNIT), BF16),
            pltpu.VMEM((3, 672, UNIT), BF16),
            pltpu.VMEM((3, TOK, UNIT), BF16),
            pltpu.VMEM((3, CH, UNIT), F32),
            pltpu.VMEM((TOK, HALF), F32),
            pltpu.VMEM((TOK, HALF), BF16),
            pltpu.VMEM((TOK, HALF), BF16),
            pltpu.VMEM((3, 4, BLK, HALF), BF16),
            pltpu.VMEM((3, 4, BLK, HALF), BF16),
            pltpu.VMEM((3, BLK, HALF), BF16),
            pltpu.VMEM((3, BLK, HALF), BF16),
            pltpu.VMEM((BLK, HALF), F32),
            pltpu.VMEM((2, 24, HALF), F32),
            pltpu.VMEM((24, HALF), F32),
            pltpu.VMEM((5, 4, 8, 128), F32),
            pltpu.VMEM((14, 4, 8, 128), F32),
            pltpu.SemaphoreType.DMA((NSEM,)),
            pltpu.SemaphoreType.DMA((NSEM,)),
            pltpu.SemaphoreType.DMA((5,)),
        ],
        compiler_params=pltpu.CompilerParams(
            collective_id=0, has_side_effects=True, vmem_limit_bytes=44 * 1024 * 1024
        ),
    )(
        saved_scale,
        gate_scale,
        up_scale,
        down_scale,
        saved_codes,
        grad_output,
        gate_codes,
        up_codes,
        down_codes,
    )
    gate_out = (gate_w / tops[0, 0]).astype(BF16)
    up_out = (up_w / tops[1, 0]).astype(BF16)
    down_out = (down_w / tops[2, 0]).astype(BF16)
    input_out = (input_w / tops[3, 0]).astype(BF16)
    return (gate_out, up_out, down_out, input_out, tops[:4, 0])


def solution(mesh):
    placed = (
        P("wide", "narrow"),
        P("wide", "narrow"),
        P("wide", "narrow"),
        P("narrow", "wide"),
        P("narrow", "wide"),
        P("narrow", "wide"),
        P("narrow", "wide"),
        P("wide", "narrow"),
        P("wide", "narrow"),
    )
    return jax.shard_map(
        per_device,
        mesh=mesh,
        in_specs=placed,
        out_specs=(
            P("narrow", "wide"),
            P("narrow", "wide"),
            P("wide", "narrow"),
            P("wide", "narrow"),
            P(),
        ),
        check_vma=False,
    )
```

```python
import jax
import jax.numpy as jnp
from jax import lax
from jax.experimental import pallas as pl
from jax.experimental.pallas import tpu as pltpu
from jax.sharding import PartitionSpec as P

eps = 1e-06
F32 = jnp.float32
BF16 = jnp.bfloat16
TOK, FEAT, UNIT = 768, 1024, 896
HALF = FEAT // 2
BLK = 48
CH = 96
N_SEND, N_RECV = 21, 73


def mm(lhs, rhs):
    return jnp.dot(lhs, rhs, preferred_element_type=F32)


def mm_last(lhs, rhs):
    return lax.dot_general(lhs, rhs, (((1,), (1,)), ((), ())), preferred_element_type=F32)


def mm_first(lhs, rhs):
    return lax.dot_general(lhs, rhs, (((0,), (0,)), ((), ())), preferred_element_type=F32)


def largest(value):
    rows, cols = value.shape
    folded = jnp.max(jnp.abs(value).reshape(rows // 8, 8, cols), axis=0)
    result = folded[:, :128]
    for start in range(128, cols, 128):
        result = jnp.maximum(result, folded[:, start : start + 128])
    return result


def kernel(
    saved_scale,
    gate_scale,
    up_scale,
    down_scale,
    saved_codes,
    grad_output,
    gate_hbm,
    up_hbm,
    down_hbm,
    gate_o,
    up_o,
    down_o,
    input_o,
    amax_o,
    gate_w,
    up_w,
    down_w,
    X,
    W,
    DN,
    E,
    SE,
    RB,
    SB,
    H,
    PRE,
    IGK,
    IGS,
    CR,
    CS,
    RA,
    BS,
    RBB,
    FS,
    FIN,
    FX,
    IGO,
    MX,
    MR,
    send_sem,
    recv_sem,
    load_sem,
):
    wide = lax.axis_index("wide")
    z = lax.axis_index("narrow")
    core = lax.rem(wide, 2)
    x = wide // 8
    y = lax.rem(wide // 2, 4)
    a = x + core * (y - x)
    b = y + core * (x - y)

    def at(da, db):
        pa = lax.rem(a + da + 4, 4)
        pb = lax.rem(b + db + 4, 4)
        return pa + core * (pb - pa), pb + core * (pa - pb)

    def dev(da, db):
        px, py = at(da, db)
        return (px * 8 + py * 2 + core, z)

    def off(da, db):
        px, py = at(da, db)
        rel = lax.rem(px * 2 + py // 2 - z + 8, 8)
        far = rel // 4
        base = (1 - far) * (672 - 192 * rel) + far * 192 * (rel - 4)
        return pl.multiple_of(base + lax.rem(py, 2) * BLK, 16)

    partner = (wide + 1 - 2 * core, z)
    right = (wide, lax.rem(z + 1, 8))
    left = (wide, lax.rem(z + 7, 8))

    loads = []
    for arr, src in ((0, gate_hbm), (1, up_hbm)):
        for half in range(2):
            loads.append(
                pltpu.make_async_copy(
                    src.at[pl.ds(half * HALF, HALF)], W.at[arr, half], load_sem.at[len(loads)]
                )
            )
    loads.append(pltpu.make_async_copy(down_hbm, DN, load_sem.at[4]))
    for load in loads:
        load.start()

    barrier = pltpu.get_barrier_semaphore()
    others = [partner]
    others += [(wide, lax.rem(z + k, 8)) for k in range(1, 8)]
    others += [dev(k, j) for k in range(4) for j in range(4) if k + j > 0]
    for other in others:
        pl.semaphore_signal(barrier, inc=1, device_id=other, device_id_type=pl.DeviceIdType.MESH)

    used = {"send": 0, "recv": 0}
    finals = []

    def new(kind):
        used[kind] += 1
        return used[kind] - 1

    def remote(src, dst, to, sends, recvs):
        return pltpu.make_async_remote_copy(
            src_ref=src,
            dst_ref=dst,
            send_sem=send_sem.at[sends],
            recv_sem=recv_sem.at[recvs],
            device_id=to,
            device_id_type=pl.DeviceIdType.MESH,
        )

    class Batch:
        def __init__(self, total):
            self.sends = new("send")
            finals.append((total, self.sends))

        def send(self, src, dst, to, recvs):
            remote(src, dst, to, self.sends, recvs).start()

    def arrived(ref, recvs):
        remote(ref, ref, partner, 0, recvs).wait_recv()

    first_core = core == 0
    tokens = [saved_codes[...].astype(F32) * saved_scale[0, 0], grad_output[...].astype(F32)]
    for t in range(2):
        low, high = tokens[t][:, :HALF], tokens[t][:, HALF:]
        E[t, core] = jnp.where(first_core, low, high)
        SE[t] = jnp.where(first_core, high, low)
    pl.semaphore_wait(barrier, len(others))
    swap = Batch(SE)
    swaps = [new("recv") for _ in range(2)]
    for t in range(2):
        swap.send(SE.at[t], E.at[t, core], partner, swaps[t])

    def gather(t):
        plane = Batch(X.at[t, 0, pl.ds(0, 720)])
        pair = Batch(X.at[t, 0])
        pair_sem = new("recv")
        across = [new("recv") for _ in range(3)]
        along = [[new("recv") for _ in range(3)] for _ in range(4)]
        order = [0, 1, 3, 2]

        def block(da, db):
            return X.at[t, core, pl.ds(off(da, db), BLK)]

        def give(da, db):
            pair.send(block(da, db), block(da, db), partner, pair_sem)

        def give_along(i):
            for k in (1, 3, 2):
                plane.send(block(order[i], 0), block(order[i], 0), dev(0, k), along[i][k - 1])
            give(order[i], 0)

        arrived(E.at[t, 0], swaps[t])
        X[t, core, pl.ds(off(0, 0), BLK)] = jnp.concatenate([E[t, 0], E[t, 1]], axis=0).astype(BF16)
        for k in (1, 3, 2):
            plane.send(block(0, 0), block(0, 0), dev(k, 0), across[k - 1])
        give_along(0)
        yield
        for i in range(1, 4):
            arrived(block(0, 0), across[3 - order[i]])
            give_along(i)
            if i > 1:
                yield
        for i in range(4):
            for k in (1, 3, 2):
                arrived(block(0, 0), along[i][3 - k])
                give(order[i], k)
            if i % 2 == 1:
                yield
        arrived(X.at[t, 0], pair_sem)

    def run(gen):
        for _ in gen:
            pass

    def step(gen):
        next(gen, None)

    run(gather(0))
    grads = gather(1)
    step(grads)

    scales = [gate_scale[0, 0], up_scale[0, 0], down_scale[0, 0]]

    def partial(arr, start, count):
        rows = pl.ds(start, count)
        if arr < 2:
            value = mm(X[0, 0, rows], W[arr, 0]) + mm(X[0, 1, rows], W[arr, 1])
        else:
            value = mm_last(X[1, 0, rows], DN[:, :HALF]) + mm_last(X[1, 1, rows], DN[:, HALF:])
        return value * scales[arr]

    def reduce(arr):
        out = Batch(SB.at[arr])
        sems = [new("recv") for _ in range(4)]

        def push(k, src, dst_right, dst_left, count=CH):
            out.send(SB.at[arr, pl.ds(src, count)], RB.at[arr, pl.ds(dst_right, count)], right, sems[k])
            src = src + count
            out.send(SB.at[arr, pl.ds(src, count)], RB.at[arr, pl.ds(dst_left, count)], left, sems[k])

        SB[arr, 0:96] = partial(arr, 0, 96).astype(BF16)
        push(0, 0, 96, 240, BLK)
        yield
        value = partial(arr, 96, 192)
        arrived(RB.at[arr, pl.ds(0, 96)], sems[0])
        SB[arr, 96:144] = (value[0:48] + RB[arr, 96:144].astype(F32)).astype(BF16)
        SB[arr, 144:240] = value[48:144].astype(BF16)
        SB[arr, 240:288] = (value[144:192] + RB[arr, 240:288].astype(F32)).astype(BF16)
        push(1, 96, 288, 384)
        yield
        for k, start in ((2, 288), (3, 480)):
            value = partial(arr, start, 192)
            arrived(RB.at[arr, pl.ds(0, 192)], sems[k - 1])
            SB[arr, start : start + 192] = (value + RB[arr, start : start + 192].astype(F32)).astype(BF16)
            push(k, start, start + 192, start + 288)
            yield
        value = partial(arr, 672, 96)
        arrived(RB.at[arr, pl.ds(0, 192)], sems[3])
        PRE[arr] = value + RB[arr, 672:768].astype(F32) + RB[arr, 768:864].astype(F32)
        yield

    def spread(arr):
        out = Batch(H.at[arr, pl.ds(0, 672)])
        sems = [new("recv") for _ in range(4)]

        def push(k, src_right, dst_right, src_left, dst_left, count=CH):
            out.send(H.at[arr, pl.ds(src_right, count)], H.at[arr, pl.ds(dst_right, count)], right, sems[k])
            out.send(H.at[arr, pl.ds(src_left, count)], H.at[arr, pl.ds(dst_left, count)], left, sems[k])

        push(0, 672, 576, 672, 480)
        yield
        arrived(H.at[arr, pl.ds(0, 192)], sems[0])
        push(1, 576, 384, 480, 288)
        yield
        arrived(H.at[arr, pl.ds(0, 192)], sems[1])
        push(2, 384, 192, 288, 96)
        yield
        arrived(H.at[arr, pl.ds(0, 192)], sems[2])
        push(3, 192, 0, 144, 48, BLK)
        yield
        arrived(H.at[arr, pl.ds(0, 96)], sems[3])
        yield

    for load in loads[:4]:
        load.wait()
    gate_sum, up_sum, hidden_sum = reduce(0), reduce(1), reduce(2)
    for _ in range(3):
        step(gate_sum)
        step(grads)
        step(up_sum)
        step(grads)
    step(gate_sum)
    step(grads)
    step(up_sum)
    run(grads)
    loads[4].wait()
    step(hidden_sum)
    step(gate_sum)
    step(up_sum)

    def hidden_rows(i, carry):
        rows = pl.ds(pl.multiple_of(i * 16, 16), 16)
        gate_pre = PRE[0, rows]
        H[0, pl.ds(pl.multiple_of(672 + i * 16, 16), 16)] = (
            gate_pre * jax.nn.sigmoid(gate_pre) * PRE[1, rows]
        ).astype(BF16)
        return carry

    lax.fori_loop(0, 6, hidden_rows, 0)
    hidden_all, gate_all, up_all = spread(0), spread(1), spread(2)
    step(hidden_all)
    for _ in range(4):
        step(hidden_sum)

    def grad_rows(i, carry):
        rows = pl.ds(pl.multiple_of(i * 16, 16), 16)
        out = pl.ds(pl.multiple_of(672 + i * 16, 16), 16)
        gate_pre = PRE[0, rows]
        hidden_grad = PRE[2, rows]
        sig = jax.nn.sigmoid(gate_pre)
        H[1, out] = (hidden_grad * PRE[1, rows] * sig * (1.0 + gate_pre * (1.0 - sig))).astype(BF16)
        H[2, out] = (hidden_grad * gate_pre * sig).astype(BF16)
        return carry

    lax.fori_loop(0, 6, grad_rows, 0)
    step(gate_all)
    step(up_all)

    def set_top(which, k, top):
        MX[which, 0, 4 * k : 4 * k + 4] = jnp.maximum(top[:4], top[4:])

    def weight_part(kind, start, count, first, last):
        def tile(i, top):
            rows = pl.ds(start, count)
            if kind < 2:
                ref = (gate_w, up_w)[kind]
                half = i // 2
                cols = pl.ds(pl.multiple_of(lax.rem(i, 2) * 256, 256), 256)
                value = mm_first(X[0, half, rows, cols], H[1 + kind, rows])
                where = pl.ds(pl.multiple_of(i * 256, 256), 256)
                if not first:
                    value = value + ref[where]
                ref[where] = value
            else:
                cols = pl.ds(pl.multiple_of(i * 128, 128), 128)
                value = jnp.concatenate(
                    [mm_first(H[0, rows, cols], X[1, half, rows]) for half in range(2)], axis=1
                )
                if not first:
                    value = value + down_w[cols]
                down_w[cols] = value
            return jnp.maximum(top, largest(value)) if last else top

        top = lax.fori_loop(0, 4 if kind < 2 else 7, tile, jnp.zeros((8, 128), F32))
        if last:
            set_top(kind // 2, kind % 2, top)

    pulls = Batch(IGS)
    pull_sems = [new("recv") for _ in range(2)]
    across = Batch(CS.at[pl.ds(0, 12)])
    across_sems = [new("recv") for _ in range(3)]

    def input_part(start, count, batch):
        rows = pl.ds(start, count)

        def half_value(half):
            return scales[0] * mm_last(H[1, rows], W[0, half]) + scales[1] * mm_last(H[2, rows], W[1, half])

        IGS[rows] = half_value(1 - core).astype(BF16)
        pulls.send(IGS.at[rows], CR.at[rows], partner, pull_sems[batch])
        IGK[rows] = half_value(core)

    def input_across(lower, upper):
        def block(r, carry):
            q = r // 2
            odd = lax.rem(q, 2)
            rel = odd * ((7 - q) // 2) + (1 - odd) * (4 + q // 2)
            c = lax.rem(z + rel, 8)
            px = c // 2
            py = 2 * lax.rem(c, 2) + lax.rem(r, 2)
            da = lax.rem(px + core * (py - px) - a + 4, 4)
            db = lax.rem(py + core * (px - py) - b + 4, 4)

            @pl.when(da != 0)
            def _():
                rows = pl.ds(pl.multiple_of(r * BLK, 16), BLK)
                slot = (da - 1) * 4 + db
                CS[slot] = (IGK[rows] + CR[rows].astype(F32)).astype(BF16)
                for k in range(1, 4):
                    @pl.when(da == k)
                    def _():
                        across.send(CS.at[slot], RA.at[slot], dev(k, 0), across_sems[k - 1])

            return carry

        lax.fori_loop(lower, upper, block, 0)

    groups = [
        [partner],
        [(wide, lax.rem(z + k, 8)) for k in range(1, 8)],
        [dev(k, j) for k in range(4) for j in range(4) if k + j > 0],
    ]

    def maxima(which):
        base = 0
        for phase, group in enumerate(groups):
            out = Batch(MR.at[which, pl.ds(0, len(group))])
            sem = new("recv")
            for k, other in enumerate(group):
                out.send(MX.at[which, phase], MR.at[which, base + k], other, sem)
            yield
            arrived(MR.at[which, pl.ds(0, len(group))], sem)
            value = MX[which, phase]
            for k in range(len(group)):
                value = jnp.maximum(value, MR[which, base + k])
            MX[which, phase + 1] = value
            base += len(group)

    def amax(which, k):
        return jnp.max(MX[which, 3, 4 * k : 4 * k + 4]) + eps

    def scaled(src, dst, top):
        inverse = 1.0 / jnp.full((16, 128), top, F32)
        rows, cols = src.shape
        factor = jnp.concatenate([inverse] * (cols // 128), axis=1)

        def tile(i, carry):
            where = pl.ds(pl.multiple_of(i * 16, 16), 16)
            dst[where] = (src[where] * factor).astype(BF16)
            return carry

        lax.fori_loop(0, rows // 16, tile, 0)

    step(gate_all)
    step(up_all)
    input_part(480, 288, 0)
    step(gate_all)
    step(up_all)
    input_part(288, 192, 0)
    step(hidden_all)
    arrived(CR.at[pl.ds(0, 480)], pull_sems[0])
    input_across(6, 16)
    weight_part(0, 288, 480, True, False)
    step(gate_all)
    step(up_all)
    input_part(96, 192, 1)
    step(hidden_all)
    weight_part(1, 288, 480, True, False)
    step(gate_all)
    step(up_all)
    input_part(0, 96, 1)
    step(hidden_all)
    weight_part(0, 0, 288, False, True)
    arrived(CR.at[pl.ds(0, 288)], pull_sems[1])
    input_across(0, 6)
    weight_part(1, 0, 288, False, True)
    first_tops = maxima(0)
    step(first_tops)
    weight_part(2, 288, 480, True, False)
    step(first_tops)
    for sem in across_sems:
        arrived(RA.at[pl.ds(0, 4)], sem)
    along = Batch(BS)
    along_sems = [new("recv") for _ in range(3)]
    for db in (2, 1, 3, 0):
        rows = pl.ds(off(0, db), BLK)
        value = IGK[rows] + CR[rows].astype(F32)
        for k in range(3):
            value = value + RA[4 * k + db].astype(F32)
        if db == 0:
            FS[...] = value
        else:
            BS[db - 1] = value.astype(BF16)
            along.send(BS.at[db - 1], RBB.at[db - 1], dev(0, db), along_sems[db - 1])
    step(hidden_all)
    step(first_tops)
    weight_part(2, 0, 288, False, True)
    value = FS[...]
    for k in range(3):
        arrived(RBB.at[0], along_sems[k])
        value = value + RBB[k].astype(F32)
    FIN[0] = value[:24]
    FIN[1] = value[24:]
    last = Batch(FX)
    last_sem = new("recv")
    last.send(FIN.at[1 - core], FX, partner, last_sem)
    run(first_tops)
    arrived(FX, last_sem)
    mine, theirs = FIN[core], FX[...]
    low = jnp.where(first_core, mine, theirs)
    high = jnp.where(first_core, theirs, mine)
    IGO[:, :HALF] = low
    IGO[:, HALF:] = high
    set_top(1, 1, jnp.maximum(largest(low), largest(high)))
    second_tops = maxima(1)
    step(second_tops)
    step(second_tops)
    scaled(gate_w, gate_o, amax(0, 0))
    step(second_tops)
    scaled(up_w, up_o, amax(0, 1))
    run(second_tops)
    scaled(down_w, down_o, amax(1, 0))
    inverse = 1.0 / jnp.full((24, 128), amax(1, 1), F32)
    input_o[...] = (IGO[...] * jnp.concatenate([inverse] * 8, axis=1)).astype(BF16)
    for k in range(4):
        amax_o[k : k + 1] = jnp.full((1, 128), amax(k // 2, k % 2), F32)
    amax_o[4:] = jnp.zeros((4, 128), F32)

    assert (used["send"], used["recv"]) == (N_SEND, N_RECV), used
    for total, sends in finals:
        remote(total, total, partner, sends, 0).wait_send()


def per_device(
    saved_codes,
    saved_scale,
    grad_output,
    gate_codes,
    gate_scale,
    up_codes,
    up_scale,
    down_codes,
    down_scale,
):
    smem = pl.BlockSpec(memory_space=pltpu.SMEM)
    vmem = pl.BlockSpec(memory_space=pltpu.VMEM)
    hbm = pl.BlockSpec(memory_space=pl.ANY)
    gate_out, up_out, down_out, input_out, tops = pl.pallas_call(
        kernel,
        out_shape=[
            pltpu.VMEM((FEAT, UNIT), BF16),
            pltpu.VMEM((FEAT, UNIT), BF16),
            pltpu.VMEM((UNIT, FEAT), BF16),
            pltpu.VMEM((24, FEAT), BF16),
            pltpu.VMEM((8, 128), F32),
        ],
        in_specs=[smem] * 4 + [vmem] * 2 + [hbm] * 3,
        out_specs=[vmem] * 5,
        scratch_shapes=[
            pltpu.VMEM((FEAT, UNIT), F32),
            pltpu.VMEM((FEAT, UNIT), F32),
            pltpu.VMEM((UNIT, FEAT), F32),
            pltpu.VMEM((2, 2, TOK, HALF), BF16),
            pltpu.VMEM((2, 2, HALF, UNIT), BF16),
            pltpu.VMEM((UNIT, FEAT), BF16),
            pltpu.VMEM((2, 2, 24, HALF), F32),
            pltpu.VMEM((2, 24, HALF), F32),
            pltpu.VMEM((3, 864, UNIT), BF16),
            pltpu.VMEM((3, 672, UNIT), BF16),
            pltpu.VMEM((3, TOK, UNIT), BF16),
            pltpu.VMEM((3, CH, UNIT), F32),
            pltpu.VMEM((TOK, HALF), F32),
            pltpu.VMEM((TOK, HALF), BF16),
            pltpu.VMEM((TOK, HALF), BF16),
            pltpu.VMEM((12, BLK, HALF), BF16),
            pltpu.VMEM((12, BLK, HALF), BF16),
            pltpu.VMEM((3, BLK, HALF), BF16),
            pltpu.VMEM((3, BLK, HALF), BF16),
            pltpu.VMEM((BLK, HALF), F32),
            pltpu.VMEM((2, 24, HALF), F32),
            pltpu.VMEM((24, HALF), F32),
            pltpu.VMEM((24, FEAT), F32),
            pltpu.VMEM((2, 4, 8, 128), F32),
            pltpu.VMEM((2, 23, 8, 128), F32),
            pltpu.SemaphoreType.DMA((N_SEND,)),
            pltpu.SemaphoreType.DMA((N_RECV,)),
            pltpu.SemaphoreType.DMA((5,)),
        ],
        compiler_params=pltpu.CompilerParams(
            collective_id=0, has_side_effects=True, vmem_limit_bytes=52 * 1024 * 1024
        ),
    )(
        saved_scale,
        gate_scale,
        up_scale,
        down_scale,
        saved_codes,
        grad_output,
        gate_codes,
        up_codes,
        down_codes,
    )
    return (gate_out, up_out, down_out, input_out, tops[:4, 0])


def solution(mesh):
    placed = (
        P("wide", "narrow"),
        P("wide", "narrow"),
        P("wide", "narrow"),
        P("narrow", "wide"),
        P("narrow", "wide"),
        P("narrow", "wide"),
        P("narrow", "wide"),
        P("wide", "narrow"),
        P("wide", "narrow"),
    )
    return jax.shard_map(
        per_device,
        mesh=mesh,
        in_specs=placed,
        out_specs=(
            P("narrow", "wide"),
            P("narrow", "wide"),
            P("wide", "narrow"),
            P("wide", "narrow"),
            P(),
        ),
        check_vma=False,
    )
```

```python
import jax
import jax.numpy as jnp
from jax import lax
from jax.experimental import pallas as pl
from jax.experimental.pallas import tpu as pltpu
from jax.sharding import PartitionSpec as P

eps = 1e-06
F32 = jnp.float32
BF16 = jnp.bfloat16
TOK, FEAT, UNIT = 768, 1024, 896
HALF = FEAT // 2
BLK = 48
CH = 96
WINDOW = 9
N_SEND, N_RECV = 15 + WINDOW, 73


def mm(lhs, rhs):
    return jnp.dot(lhs, rhs, preferred_element_type=F32)


def mm_last(lhs, rhs):
    return lax.dot_general(lhs, rhs, (((1,), (1,)), ((), ())), preferred_element_type=F32)


def mm_first(lhs, rhs):
    return lax.dot_general(lhs, rhs, (((0,), (0,)), ((), ())), preferred_element_type=F32)


def largest(value):
    rows, cols = value.shape
    folded = jnp.max(jnp.abs(value).reshape(rows // 8, 8, cols), axis=0)
    result = folded[:, :128]
    for start in range(128, cols, 128):
        result = jnp.maximum(result, folded[:, start : start + 128])
    return result


def kernel(
    saved_scale,
    gate_scale,
    up_scale,
    down_scale,
    saved_codes,
    grad_output,
    gate_hbm,
    up_hbm,
    down_hbm,
    gate_o,
    up_o,
    down_o,
    input_o,
    amax_o,
    gate_w,
    up_w,
    down_w,
    X,
    W,
    DN,
    E,
    SE,
    RB,
    SB,
    RF,
    SF,
    H,
    PRE,
    AHEAD,
    IGK,
    IGS,
    CR,
    CS,
    RA,
    BS,
    RBB,
    FS,
    FIN,
    FX,
    IGO,
    MX,
    MR,
    send_sem,
    recv_sem,
    load_sem,
):
    wide = lax.axis_index("wide")
    z = lax.axis_index("narrow")
    core = lax.rem(wide, 2)
    x = wide // 8
    y = lax.rem(wide // 2, 4)
    a = x + core * (y - x)
    b = y + core * (x - y)

    def at(da, db):
        pa = lax.rem(a + da + 4, 4)
        pb = lax.rem(b + db + 4, 4)
        return pa + core * (pb - pa), pb + core * (pa - pb)

    def dev(da, db):
        px, py = at(da, db)
        return (px * 8 + py * 2 + core, z)

    def off(da, db):
        px, py = at(da, db)
        rel = lax.rem(px * 2 + py // 2 - z + 8, 8)
        far = rel // 4
        base = (1 - far) * (672 - 192 * rel) + far * 192 * (rel - 4)
        return pl.multiple_of(base + lax.rem(py, 2) * BLK, 16)

    partner = (wide + 1 - 2 * core, z)
    right = (wide, lax.rem(z + 1, 8))
    left = (wide, lax.rem(z + 7, 8))

    loads = []
    for arr, src in ((0, gate_hbm), (1, up_hbm)):
        for half in range(2):
            loads.append(
                pltpu.make_async_copy(
                    src.at[pl.ds(half * HALF, HALF)], W.at[arr, half], load_sem.at[len(loads)]
                )
            )
    loads.append(pltpu.make_async_copy(down_hbm, DN, load_sem.at[4]))
    for load in loads:
        load.start()

    barrier = pltpu.get_barrier_semaphore()
    others = [partner]
    others += [(wide, lax.rem(z + k, 8)) for k in range(1, 8)]
    others += [dev(k, j) for k in range(4) for j in range(4) if k + j > 0]
    for other in others:
        pl.semaphore_signal(barrier, inc=1, device_id=other, device_id_type=pl.DeviceIdType.MESH)

    used = {"send": 0, "recv": 0}
    finals = []

    def new(kind):
        used[kind] += 1
        return used[kind] - 1

    def remote(src, dst, to, sends, recvs):
        return pltpu.make_async_remote_copy(
            src_ref=src,
            dst_ref=dst,
            send_sem=send_sem.at[sends],
            recv_sem=recv_sem.at[recvs],
            device_id=to,
            device_id_type=pl.DeviceIdType.MESH,
        )

    class Batch:
        def __init__(self, total):
            self.sends = new("send")
            finals.append((total, self.sends))

        def send(self, src, dst, to, recvs):
            remote(src, dst, to, self.sends, recvs).start()

    z_free = [new("send") for _ in range(WINDOW)]
    z_last = []

    def z_left(most):
        while len(z_last) > most:
            ref, sem = z_last.pop(0)
            remote(ref, ref, partner, sem, 0).wait_send()
            z_free.append(sem)

    def z_push(total, to_right, to_left, recvs):
        z_left(WINDOW - 1)
        sem = z_free.pop(0)
        remote(*to_right, right, sem, recvs).start()
        remote(*to_left, left, sem, recvs).start()
        z_last.append((total, sem))

    def arrived(ref, recvs):
        remote(ref, ref, partner, 0, recvs).wait_recv()

    first_core = core == 0
    tokens = [saved_codes[...].astype(F32) * saved_scale[0, 0], grad_output[...].astype(F32)]
    for t in range(2):
        low, high = tokens[t][:, :HALF], tokens[t][:, HALF:]
        E[t, core] = jnp.where(first_core, low, high)
        SE[t] = jnp.where(first_core, high, low)
    pl.semaphore_wait(barrier, len(others))
    swap = Batch(SE)
    swaps = [new("recv") for _ in range(2)]
    for t in range(2):
        swap.send(SE.at[t], E.at[t, core], partner, swaps[t])

    def gather(t):
        plane = Batch(X.at[t, 0, pl.ds(0, 720)])
        pair = Batch(X.at[t, 0])
        pair_sem = new("recv")
        across = [new("recv") for _ in range(3)]
        along = [[new("recv") for _ in range(3)] for _ in range(4)]
        order = [0, 1, 3, 2]

        def block(da, db):
            return X.at[t, core, pl.ds(off(da, db), BLK)]

        def give(da, db):
            pair.send(block(da, db), block(da, db), partner, pair_sem)

        def give_along(i):
            for k in (1, 3, 2):
                plane.send(block(order[i], 0), block(order[i], 0), dev(0, k), along[i][k - 1])
            give(order[i], 0)

        arrived(E.at[t, 0], swaps[t])
        X[t, core, pl.ds(off(0, 0), BLK)] = jnp.concatenate([E[t, 0], E[t, 1]], axis=0).astype(BF16)
        for k in (1, 3, 2):
            plane.send(block(0, 0), block(0, 0), dev(k, 0), across[k - 1])
        give_along(0)
        yield
        for i in range(1, 4):
            arrived(block(0, 0), across[3 - order[i]])
            give_along(i)
            if i > 1:
                yield
        for i in range(4):
            for k in (1, 3, 2):
                arrived(block(0, 0), along[i][3 - k])
                give(order[i], k)
            if i % 2 == 1:
                yield
        arrived(X.at[t, 0], pair_sem)

    def run(gen):
        for _ in gen:
            pass

    def step(gen):
        next(gen, None)

    run(gather(0))
    grads = gather(1)
    step(grads)

    scales = [gate_scale[0, 0], up_scale[0, 0], down_scale[0, 0]]

    def partial(arr, start, count):
        rows = pl.ds(start, count)
        if arr < 2:
            value = mm(X[0, 0, rows], W[arr, 0]) + mm(X[0, 1, rows], W[arr, 1])
        else:
            value = mm_last(X[1, 0, rows], DN[:, :HALF]) + mm_last(X[1, 1, rows], DN[:, HALF:])
        return value * scales[arr]

    def reduce(arr):
        sems = [new("recv") for _ in range(4)]

        def push(k, src, dst_right, dst_left, count=CH):
            z_push(
                SB.at[arr, pl.ds(src, 2 * count)],
                (SB.at[arr, pl.ds(src, count)], RB.at[arr, pl.ds(dst_right, count)]),
                (SB.at[arr, pl.ds(src + count, count)], RB.at[arr, pl.ds(dst_left, count)]),
                sems[k],
            )

        SB[arr, 0:96] = partial(arr, 0, 96).astype(BF16)
        push(0, 0, 96, 240, BLK)
        yield
        if arr == 0:
            for start, count in ((96, 192), (288, 192), (480, 192), (672, 96)):
                AHEAD[start - 96 : start - 96 + count] = partial(arr, start, count)
            yield

        def part(start, count):
            return AHEAD[start - 96 : start - 96 + count] if arr == 0 else partial(arr, start, count)

        value = part(96, 192)
        arrived(RB.at[arr, pl.ds(0, 96)], sems[0])
        SB[arr, 96:144] = (value[0:48] + RB[arr, 96:144].astype(F32)).astype(BF16)
        SB[arr, 144:240] = value[48:144].astype(BF16)
        SB[arr, 240:288] = (value[144:192] + RB[arr, 240:288].astype(F32)).astype(BF16)
        push(1, 96, 288, 384)
        yield
        for k, start, got in ((2, 288, RB.at[arr, 288:480]), (3, 480, RF.at[arr, 0:192])):
            value = part(start, 192)
            arrived(got, sems[k - 1])
            src = start - 288
            SF[arr, src : src + 192] = value + got[...].astype(F32)
            z_push(
                SF.at[arr, pl.ds(src, 192)],
                (SF.at[arr, pl.ds(src, CH)], RF.at[arr, pl.ds(src, CH)]),
                (SF.at[arr, pl.ds(src + CH, CH)], RF.at[arr, pl.ds(src + CH, CH)]),
                sems[k],
            )
            yield
        value = part(672, 96)
        arrived(RF.at[arr, 192:384], sems[3])
        PRE[arr] = value + RF[arr, 192:288] + RF[arr, 288:384]
        yield

    def spread(arr):
        sems = [new("recv") for _ in range(4)]

        def push(k, src_right, dst_right, src_left, dst_left, count=CH):
            z_push(
                H.at[arr, pl.ds(0, 2 * count)],
                (H.at[arr, pl.ds(src_right, count)], H.at[arr, pl.ds(dst_right, count)]),
                (H.at[arr, pl.ds(src_left, count)], H.at[arr, pl.ds(dst_left, count)]),
                sems[k],
            )

        push(0, 672, 576, 672, 480)
        yield
        arrived(H.at[arr, pl.ds(0, 192)], sems[0])
        push(1, 576, 384, 480, 288)
        yield
        arrived(H.at[arr, pl.ds(0, 192)], sems[1])
        push(2, 384, 192, 288, 96)
        yield
        arrived(H.at[arr, pl.ds(0, 192)], sems[2])
        push(3, 192, 0, 144, 48, BLK)
        yield
        arrived(H.at[arr, pl.ds(0, 96)], sems[3])
        yield

    for load in loads[:4]:
        load.wait()
    gate_sum, up_sum, hidden_sum = reduce(0), reduce(1), reduce(2)
    step(gate_sum)
    step(gate_sum)
    step(up_sum)
    step(gate_sum)
    step(grads)
    step(up_sum)
    step(grads)
    step(grads)
    step(gate_sum)
    run(grads)
    loads[4].wait()
    step(hidden_sum)
    step(up_sum)
    step(hidden_sum)
    step(gate_sum)
    step(up_sum)
    step(hidden_sum)
    step(gate_sum)
    step(up_sum)

    def hidden_rows(i, carry):
        rows = pl.ds(pl.multiple_of(i * 16, 16), 16)
        gate_pre = PRE[0, rows]
        H[0, pl.ds(pl.multiple_of(672 + i * 16, 16), 16)] = (
            gate_pre * jax.nn.sigmoid(gate_pre) * PRE[1, rows]
        ).astype(BF16)
        return carry

    lax.fori_loop(0, 6, hidden_rows, 0)
    hidden_all, gate_all, up_all = spread(0), spread(1), spread(2)
    step(hidden_all)
    step(hidden_sum)
    step(hidden_all)
    step(hidden_sum)

    def gate_rows(i, carry):
        rows = pl.ds(pl.multiple_of(i * 16, 16), 16)
        gate_pre = PRE[0, rows]
        sig = jax.nn.sigmoid(gate_pre)
        H[1, pl.ds(pl.multiple_of(672 + i * 16, 16), 16)] = (
            PRE[2, rows] * PRE[1, rows] * sig * (1.0 + gate_pre * (1.0 - sig))
        ).astype(BF16)
        return carry

    def up_rows(i, carry):
        rows = pl.ds(pl.multiple_of(i * 16, 16), 16)
        gate_pre = PRE[0, rows]
        H[2, pl.ds(pl.multiple_of(672 + i * 16, 16), 16)] = (
            PRE[2, rows] * gate_pre * jax.nn.sigmoid(gate_pre)
        ).astype(BF16)
        return carry

    lax.fori_loop(0, 6, gate_rows, 0)
    step(gate_all)
    lax.fori_loop(0, 6, up_rows, 0)

    def set_top(which, k, top):
        MX[which, 0, 4 * k : 4 * k + 4] = jnp.maximum(top[:4], top[4:])

    def weight_part(kind, start, count, first, last):
        def tile(i, top):
            rows = pl.ds(start, count)
            if kind < 2:
                ref = (gate_w, up_w)[kind]
                half = i // 2
                cols = pl.ds(pl.multiple_of(lax.rem(i, 2) * 256, 256), 256)
                value = mm_first(X[0, half, rows, cols], H[1 + kind, rows])
                where = pl.ds(pl.multiple_of(i * 256, 256), 256)
                if not first:
                    value = value + ref[where]
                ref[where] = value
            else:
                cols = pl.ds(pl.multiple_of(i * 128, 128), 128)
                value = jnp.concatenate(
                    [mm_first(H[0, rows, cols], X[1, half, rows]) for half in range(2)], axis=1
                )
                if not first:
                    value = value + down_w[cols]
                down_w[cols] = value
            return jnp.maximum(top, largest(value)) if last else top

        top = lax.fori_loop(0, 4 if kind < 2 else 7, tile, jnp.zeros((8, 128), F32))
        if last:
            set_top(kind // 2, kind % 2, top)

    pulls = Batch(IGS)
    pull_sems = [new("recv") for _ in range(2)]
    across = Batch(CS.at[pl.ds(0, 12)])
    across_sems = [new("recv") for _ in range(3)]

    def input_part(start, count, batch):
        rows = pl.ds(start, count)

        def half_value(half):
            return scales[0] * mm_last(H[1, rows], W[0, half]) + scales[1] * mm_last(H[2, rows], W[1, half])

        IGS[rows] = half_value(1 - core).astype(BF16)
        pulls.send(IGS.at[rows], CR.at[rows], partner, pull_sems[batch])
        IGK[rows] = half_value(core)

    def input_across(lower, upper):
        def block(r, carry):
            q = r // 2
            odd = lax.rem(q, 2)
            rel = odd * ((7 - q) // 2) + (1 - odd) * (4 + q // 2)
            c = lax.rem(z + rel, 8)
            px = c // 2
            py = 2 * lax.rem(c, 2) + lax.rem(r, 2)
            da = lax.rem(px + core * (py - px) - a + 4, 4)
            db = lax.rem(py + core * (px - py) - b + 4, 4)

            @pl.when(da != 0)
            def _():
                rows = pl.ds(pl.multiple_of(r * BLK, 16), BLK)
                slot = (da - 1) * 4 + db
                CS[slot] = (IGK[rows] + CR[rows].astype(F32)).astype(BF16)
                for k in range(1, 4):
                    @pl.when(da == k)
                    def _():
                        across.send(CS.at[slot], RA.at[slot], dev(k, 0), across_sems[k - 1])

            return carry

        lax.fori_loop(lower, upper, block, 0)

    groups = [
        [partner],
        [(wide, lax.rem(z + k, 8)) for k in range(1, 8)],
        [dev(k, j) for k in range(4) for j in range(4) if k + j > 0],
    ]

    def maxima(which):
        base = 0
        for phase, group in enumerate(groups):
            out = Batch(MR.at[which, pl.ds(0, len(group))])
            sem = new("recv")
            for k, other in enumerate(group):
                out.send(MX.at[which, phase], MR.at[which, base + k], other, sem)
            yield
            arrived(MR.at[which, pl.ds(0, len(group))], sem)
            value = MX[which, phase]
            for k in range(len(group)):
                value = jnp.maximum(value, MR[which, base + k])
            MX[which, phase + 1] = value
            base += len(group)

    def amax(which, k):
        return jnp.max(MX[which, 3, 4 * k : 4 * k + 4]) + eps

    def scaled(src, dst, top):
        inverse = 1.0 / jnp.full((16, 128), top, F32)
        rows, cols = src.shape
        factor = jnp.concatenate([inverse] * (cols // 128), axis=1)

        def tile(i, carry):
            where = pl.ds(pl.multiple_of(i * 16, 16), 16)
            dst[where] = (src[where] * factor).astype(BF16)
            return carry

        lax.fori_loop(0, rows // 16, tile, 0)

    weight_part(2, 480, 288, True, False)
    step(up_all)
    step(gate_all)
    step(up_all)
    input_part(480, 288, 0)
    step(gate_all)
    step(up_all)
    input_part(288, 192, 0)
    weight_part(0, 288, 480, True, False)
    arrived(CR.at[pl.ds(0, 480)], pull_sems[0])
    input_across(6, 16)
    step(gate_all)
    step(up_all)
    input_part(96, 192, 1)
    weight_part(1, 288, 480, True, False)
    step(gate_all)
    step(up_all)
    input_part(0, 96, 1)
    step(hidden_all)
    weight_part(0, 0, 288, False, True)
    arrived(CR.at[pl.ds(0, 288)], pull_sems[1])
    input_across(0, 6)
    weight_part(1, 0, 288, False, True)
    step(hidden_all)
    first_tops = maxima(0)
    step(first_tops)
    weight_part(2, 288, 192, False, False)
    step(first_tops)
    for sem in across_sems:
        arrived(RA.at[pl.ds(0, 4)], sem)
    along = Batch(BS)
    along_sems = [new("recv") for _ in range(3)]
    for db in (2, 1, 3, 0):
        rows = pl.ds(off(0, db), BLK)
        value = IGK[rows] + CR[rows].astype(F32)
        for k in range(3):
            value = value + RA[4 * k + db].astype(F32)
        if db == 0:
            FS[...] = value
        else:
            BS[db - 1] = value.astype(BF16)
            along.send(BS.at[db - 1], RBB.at[db - 1], dev(0, db), along_sems[db - 1])
    step(hidden_all)
    weight_part(2, 0, 288, False, True)
    value = FS[...]
    for k in range(3):
        arrived(RBB.at[0], along_sems[k])
        value = value + RBB[k].astype(F32)
    FIN[0] = value[:24]
    FIN[1] = value[24:]
    set_top(1, 1, largest(value))
    second_tops = maxima(1)
    step(second_tops)
    last = Batch(FX)
    last_sem = new("recv")
    last.send(FIN.at[1 - core], FX, partner, last_sem)
    step(second_tops)
    step(first_tops)
    run(first_tops)
    scaled(gate_w, gate_o, amax(0, 0))
    step(second_tops)
    scaled(up_w, up_o, amax(0, 1))
    arrived(FX, last_sem)
    mine, theirs = FIN[core], FX[...]
    IGO[:, :HALF] = jnp.where(first_core, mine, theirs)
    IGO[:, HALF:] = jnp.where(first_core, theirs, mine)
    run(second_tops)
    scaled(down_w, down_o, amax(1, 0))
    inverse = 1.0 / jnp.full((24, 128), amax(1, 1), F32)
    input_o[...] = (IGO[...] * jnp.concatenate([inverse] * 8, axis=1)).astype(BF16)
    for k in range(4):
        amax_o[k : k + 1] = jnp.full((1, 128), amax(k // 2, k % 2), F32)
    amax_o[4:] = jnp.zeros((4, 128), F32)

    z_left(0)
    assert (used["send"], used["recv"]) == (N_SEND, N_RECV), used
    for total, sends in finals:
        remote(total, total, partner, sends, 0).wait_send()


def per_device(
    saved_codes,
    saved_scale,
    grad_output,
    gate_codes,
    gate_scale,
    up_codes,
    up_scale,
    down_codes,
    down_scale,
):
    smem = pl.BlockSpec(memory_space=pltpu.SMEM)
    vmem = pl.BlockSpec(memory_space=pltpu.VMEM)
    hbm = pl.BlockSpec(memory_space=pl.ANY)
    gate_out, up_out, down_out, input_out, tops = pl.pallas_call(
        kernel,
        out_shape=[
            pltpu.VMEM((FEAT, UNIT), BF16),
            pltpu.VMEM((FEAT, UNIT), BF16),
            pltpu.VMEM((UNIT, FEAT), BF16),
            pltpu.VMEM((24, FEAT), BF16),
            pltpu.VMEM((8, 128), F32),
        ],
        in_specs=[smem] * 4 + [vmem] * 2 + [hbm] * 3,
        out_specs=[vmem] * 5,
        scratch_shapes=[
            pltpu.VMEM((FEAT, UNIT), F32),
            pltpu.VMEM((FEAT, UNIT), F32),
            pltpu.VMEM((UNIT, FEAT), F32),
            pltpu.VMEM((2, 2, TOK, HALF), BF16),
            pltpu.VMEM((2, 2, HALF, UNIT), BF16),
            pltpu.VMEM((UNIT, FEAT), BF16),
            pltpu.VMEM((2, 2, 24, HALF), F32),
            pltpu.VMEM((2, 24, HALF), F32),
            pltpu.VMEM((3, 480, UNIT), BF16),
            pltpu.VMEM((3, 288, UNIT), BF16),
            pltpu.VMEM((3, 384, UNIT), F32),
            pltpu.VMEM((3, 384, UNIT), F32),
            pltpu.VMEM((3, TOK, UNIT), BF16),
            pltpu.VMEM((3, CH, UNIT), F32),
            pltpu.VMEM((672, UNIT), F32),
            pltpu.VMEM((TOK, HALF), F32),
            pltpu.VMEM((TOK, HALF), BF16),
            pltpu.VMEM((TOK, HALF), BF16),
            pltpu.VMEM((12, BLK, HALF), BF16),
            pltpu.VMEM((12, BLK, HALF), BF16),
            pltpu.VMEM((3, BLK, HALF), BF16),
            pltpu.VMEM((3, BLK, HALF), BF16),
            pltpu.VMEM((BLK, HALF), F32),
            pltpu.VMEM((2, 24, HALF), F32),
            pltpu.VMEM((24, HALF), F32),
            pltpu.VMEM((24, FEAT), F32),
            pltpu.VMEM((2, 4, 8, 128), F32),
            pltpu.VMEM((2, 23, 8, 128), F32),
            pltpu.SemaphoreType.DMA((N_SEND,)),
            pltpu.SemaphoreType.DMA((N_RECV,)),
            pltpu.SemaphoreType.DMA((5,)),
        ],
        compiler_params=pltpu.CompilerParams(
            collective_id=0, has_side_effects=True, vmem_limit_bytes=54 * 1024 * 1024
        ),
    )(
        saved_scale,
        gate_scale,
        up_scale,
        down_scale,
        saved_codes,
        grad_output,
        gate_codes,
        up_codes,
        down_codes,
    )
    return (gate_out, up_out, down_out, input_out, tops[:4, 0])


def solution(mesh):
    placed = (
        P("wide", "narrow"),
        P("wide", "narrow"),
        P("wide", "narrow"),
        P("narrow", "wide"),
        P("narrow", "wide"),
        P("narrow", "wide"),
        P("narrow", "wide"),
        P("wide", "narrow"),
        P("wide", "narrow"),
    )
    return jax.shard_map(
        per_device,
        mesh=mesh,
        in_specs=placed,
        out_specs=(
            P("narrow", "wide"),
            P("narrow", "wide"),
            P("wide", "narrow"),
            P("wide", "narrow"),
            P(),
        ),
        check_vma=False,
    )
```

```python
import jax
import jax.numpy as jnp
from jax import lax
from jax.experimental import pallas as pl
from jax.experimental.pallas import tpu as pltpu
from jax.sharding import PartitionSpec as P

eps = 1e-06
F32 = jnp.float32
BF16 = jnp.bfloat16
TOK, FEAT, UNIT = 768, 1024, 896
HALF = FEAT // 2
BLK = 48
CH = 96
WINDOW = 9
N_SEND, N_RECV = 15 + WINDOW, 73


def mm(lhs, rhs):
    return jnp.dot(lhs, rhs, preferred_element_type=F32)


def mm_last(lhs, rhs):
    return lax.dot_general(lhs, rhs, (((1,), (1,)), ((), ())), preferred_element_type=F32)


def mm_first(lhs, rhs):
    return lax.dot_general(lhs, rhs, (((0,), (0,)), ((), ())), preferred_element_type=F32)


def largest(value):
    rows, cols = value.shape
    folded = jnp.max(jnp.abs(value).reshape(rows // 8, 8, cols), axis=0)
    result = folded[:, :128]
    for start in range(128, cols, 128):
        result = jnp.maximum(result, folded[:, start : start + 128])
    return result


def kernel(
    saved_scale,
    gate_scale,
    up_scale,
    down_scale,
    saved_codes,
    grad_output,
    gate_hbm,
    up_hbm,
    down_hbm,
    gate_o,
    up_o,
    down_o,
    input_o,
    amax_o,
    gate_w,
    up_w,
    down_w,
    X,
    W,
    DN,
    E,
    SE,
    RB,
    SB,
    RF,
    SF,
    H,
    PRE,
    AHEAD,
    IGK,
    IGS,
    CR,
    CS,
    RA,
    BS,
    RBB,
    FS,
    FIN,
    FX,
    IGO,
    MX,
    MR,
    send_sem,
    recv_sem,
    load_sem,
):
    wide = lax.axis_index("wide")
    z = lax.axis_index("narrow")
    core = lax.rem(wide, 2)
    x = wide // 8
    y = lax.rem(wide // 2, 4)
    a = x + core * (y - x)
    b = y + core * (x - y)

    def at(da, db):
        pa = lax.rem(a + da + 4, 4)
        pb = lax.rem(b + db + 4, 4)
        return pa + core * (pb - pa), pb + core * (pa - pb)

    def dev(da, db):
        px, py = at(da, db)
        return (px * 8 + py * 2 + core, z)

    def off(da, db):
        px, py = at(da, db)
        rel = lax.rem(px * 2 + py // 2 - z + 8, 8)
        far = rel // 4
        base = (1 - far) * (672 - 192 * rel) + far * 192 * (rel - 4)
        return pl.multiple_of(base + lax.rem(py, 2) * BLK, 16)

    partner = (wide + 1 - 2 * core, z)
    right = (wide, lax.rem(z + 1, 8))
    left = (wide, lax.rem(z + 7, 8))

    loads = []
    for arr, src in ((0, gate_hbm), (1, up_hbm)):
        for half in range(2):
            loads.append(
                pltpu.make_async_copy(
                    src.at[pl.ds(half * HALF, HALF)], W.at[arr, half], load_sem.at[len(loads)]
                )
            )
    loads.append(pltpu.make_async_copy(down_hbm, DN, load_sem.at[4]))
    for load in loads:
        load.start()

    barrier = pltpu.get_barrier_semaphore()
    others = [partner]
    others += [(wide, lax.rem(z + k, 8)) for k in range(1, 8)]
    others += [dev(k, j) for k in range(4) for j in range(4) if k + j > 0]
    for other in others:
        pl.semaphore_signal(barrier, inc=1, device_id=other, device_id_type=pl.DeviceIdType.MESH)

    used = {"send": 0, "recv": 0}
    finals = []

    def new(kind):
        used[kind] += 1
        return used[kind] - 1

    def remote(src, dst, to, sends, recvs):
        return pltpu.make_async_remote_copy(
            src_ref=src,
            dst_ref=dst,
            send_sem=send_sem.at[sends],
            recv_sem=recv_sem.at[recvs],
            device_id=to,
            device_id_type=pl.DeviceIdType.MESH,
        )

    class Batch:
        def __init__(self, total):
            self.sends = new("send")
            finals.append((total, self.sends))

        def send(self, src, dst, to, recvs):
            remote(src, dst, to, self.sends, recvs).start()

    z_free = [new("send") for _ in range(WINDOW)]
    z_last = []

    def z_left(most):
        while len(z_last) > most:
            ref, sem = z_last.pop(0)
            remote(ref, ref, partner, sem, 0).wait_send()
            z_free.append(sem)

    def z_push(total, to_right, to_left, recvs):
        z_left(WINDOW - 1)
        sem = z_free.pop(0)
        remote(*to_right, right, sem, recvs).start()
        remote(*to_left, left, sem, recvs).start()
        z_last.append((total, sem))

    def arrived(ref, recvs):
        remote(ref, ref, partner, 0, recvs).wait_recv()

    first_core = core == 0
    tokens = [saved_codes[...].astype(F32) * saved_scale[0, 0], grad_output[...].astype(F32)]
    for t in range(2):
        low, high = tokens[t][:, :HALF], tokens[t][:, HALF:]
        E[t, core] = jnp.where(first_core, low, high)
        SE[t] = jnp.where(first_core, high, low)
    pl.semaphore_wait(barrier, len(others))
    swap = Batch(SE)
    swaps = [new("recv") for _ in range(2)]
    for t in range(2):
        swap.send(SE.at[t], E.at[t, core], partner, swaps[t])

    def gather(t):
        plane = Batch(X.at[t, 0, pl.ds(0, 720)])
        pair = Batch(X.at[t, 0])
        pair_sem = new("recv")
        across = [new("recv") for _ in range(3)]
        along = [[new("recv") for _ in range(3)] for _ in range(4)]
        order = [0, 1, 3, 2]

        def block(da, db):
            return X.at[t, core, pl.ds(off(da, db), BLK)]

        def give(da, db):
            pair.send(block(da, db), block(da, db), partner, pair_sem)

        def give_along(i):
            for k in (1, 3, 2):
                plane.send(block(order[i], 0), block(order[i], 0), dev(0, k), along[i][k - 1])
            give(order[i], 0)

        arrived(E.at[t, 0], swaps[t])
        X[t, core, pl.ds(off(0, 0), BLK)] = jnp.concatenate([E[t, 0], E[t, 1]], axis=0).astype(BF16)
        for k in (1, 3, 2):
            plane.send(block(0, 0), block(0, 0), dev(k, 0), across[k - 1])
        give_along(0)
        yield
        for i in range(1, 4):
            arrived(block(0, 0), across[3 - order[i]])
            give_along(i)
            if i > 1:
                yield
        for i in range(4):
            for k in (1, 3, 2):
                arrived(block(0, 0), along[i][3 - k])
                give(order[i], k)
            if i % 2 == 1:
                yield
        arrived(X.at[t, 0], pair_sem)

    def run(gen):
        for _ in gen:
            pass

    def step(gen):
        next(gen, None)

    run(gather(0))
    grads = gather(1)
    step(grads)

    scales = [gate_scale[0, 0], up_scale[0, 0], down_scale[0, 0]]

    def partial(arr, start, count):
        rows = pl.ds(start, count)
        if arr < 2:
            value = mm(X[0, 0, rows], W[arr, 0]) + mm(X[0, 1, rows], W[arr, 1])
        else:
            value = mm_last(X[1, 0, rows], DN[:, :HALF]) + mm_last(X[1, 1, rows], DN[:, HALF:])
        return value * scales[arr]

    def reduce(arr):
        sems = [new("recv") for _ in range(4)]

        def push(k, src, dst_right, dst_left, count=CH):
            z_push(
                SB.at[arr, pl.ds(src, 2 * count)],
                (SB.at[arr, pl.ds(src, count)], RB.at[arr, pl.ds(dst_right, count)]),
                (SB.at[arr, pl.ds(src + count, count)], RB.at[arr, pl.ds(dst_left, count)]),
                sems[k],
            )

        SB[arr, 0:96] = partial(arr, 0, 96).astype(BF16)
        push(0, 0, 96, 240, BLK)
        yield
        if arr == 0:
            for start, count in ((96, 192), (288, 192), (480, 192), (672, 96)):
                AHEAD[start - 96 : start - 96 + count] = partial(arr, start, count)
            yield

        def part(start, count):
            return AHEAD[start - 96 : start - 96 + count] if arr == 0 else partial(arr, start, count)

        value = part(96, 192)
        arrived(RB.at[arr, pl.ds(0, 96)], sems[0])
        SB[arr, 96:144] = (value[0:48] + RB[arr, 96:144].astype(F32)).astype(BF16)
        SB[arr, 144:240] = value[48:144].astype(BF16)
        SB[arr, 240:288] = (value[144:192] + RB[arr, 240:288].astype(F32)).astype(BF16)
        push(1, 96, 288, 384)
        yield
        value = part(288, 192)
        arrived(RB.at[arr, pl.ds(0, 192)], sems[1])
        SB[arr, 288:480] = (value + RB[arr, 288:480].astype(F32)).astype(BF16)
        push(2, 288, 480, 576)
        yield
        value = part(480, 192)
        arrived(RB.at[arr, pl.ds(0, 192)], sems[2])
        SF[arr] = value + RB[arr, 480:672].astype(F32)
        z_push(
            SF.at[arr],
            (SF.at[arr, pl.ds(0, CH)], RF.at[arr, pl.ds(0, CH)]),
            (SF.at[arr, pl.ds(CH, CH)], RF.at[arr, pl.ds(CH, CH)]),
            sems[3],
        )
        yield
        value = part(672, 96)
        arrived(RF.at[arr], sems[3])
        PRE[arr] = value + RF[arr, 0:96] + RF[arr, 96:192]
        yield

    def spread(arr):
        sems = [new("recv") for _ in range(4)]

        def push(k, src_right, dst_right, src_left, dst_left, count=CH):
            z_push(
                H.at[arr, pl.ds(0, 2 * count)],
                (H.at[arr, pl.ds(src_right, count)], H.at[arr, pl.ds(dst_right, count)]),
                (H.at[arr, pl.ds(src_left, count)], H.at[arr, pl.ds(dst_left, count)]),
                sems[k],
            )

        push(0, 672, 576, 672, 480)
        yield
        arrived(H.at[arr, pl.ds(0, 192)], sems[0])
        push(1, 576, 384, 480, 288)
        yield
        arrived(H.at[arr, pl.ds(0, 192)], sems[1])
        push(2, 384, 192, 288, 96)
        yield
        arrived(H.at[arr, pl.ds(0, 192)], sems[2])
        push(3, 192, 0, 144, 48, BLK)
        yield
        arrived(H.at[arr, pl.ds(0, 96)], sems[3])
        yield

    for load in loads[:4]:
        load.wait()
    gate_sum, up_sum, hidden_sum = reduce(0), reduce(1), reduce(2)
    step(gate_sum)
    step(gate_sum)
    step(up_sum)
    step(gate_sum)
    step(grads)
    step(up_sum)
    step(grads)
    step(grads)
    step(gate_sum)
    run(grads)
    loads[4].wait()
    step(hidden_sum)
    step(up_sum)
    step(hidden_sum)
    step(gate_sum)
    step(up_sum)
    step(hidden_sum)
    step(gate_sum)
    step(up_sum)

    def hidden_rows(i, carry):
        rows = pl.ds(pl.multiple_of(i * 16, 16), 16)
        gate_pre = PRE[0, rows]
        H[0, pl.ds(pl.multiple_of(672 + i * 16, 16), 16)] = (
            gate_pre * jax.nn.sigmoid(gate_pre) * PRE[1, rows]
        ).astype(BF16)
        return carry

    lax.fori_loop(0, 6, hidden_rows, 0)
    hidden_all, gate_all, up_all = spread(0), spread(1), spread(2)
    step(hidden_all)
    step(hidden_sum)
    step(hidden_all)
    step(hidden_sum)

    def gate_rows(i, carry):
        rows = pl.ds(pl.multiple_of(i * 16, 16), 16)
        gate_pre = PRE[0, rows]
        sig = jax.nn.sigmoid(gate_pre)
        H[1, pl.ds(pl.multiple_of(672 + i * 16, 16), 16)] = (
            PRE[2, rows] * PRE[1, rows] * sig * (1.0 + gate_pre * (1.0 - sig))
        ).astype(BF16)
        return carry

    def up_rows(i, carry):
        rows = pl.ds(pl.multiple_of(i * 16, 16), 16)
        gate_pre = PRE[0, rows]
        H[2, pl.ds(pl.multiple_of(672 + i * 16, 16), 16)] = (
            PRE[2, rows] * gate_pre * jax.nn.sigmoid(gate_pre)
        ).astype(BF16)
        return carry

    lax.fori_loop(0, 6, gate_rows, 0)
    step(gate_all)
    lax.fori_loop(0, 6, up_rows, 0)

    def set_top(which, k, top):
        MX[which, 0, 4 * k : 4 * k + 4] = jnp.maximum(top[:4], top[4:])

    def weight_part(kind, start, count, first, last):
        def tile(i, top):
            rows = pl.ds(start, count)
            if kind < 2:
                ref = (gate_w, up_w)[kind]
                half = i // 2
                cols = pl.ds(pl.multiple_of(lax.rem(i, 2) * 256, 256), 256)
                value = mm_first(X[0, half, rows, cols], H[1 + kind, rows])
                where = pl.ds(pl.multiple_of(i * 256, 256), 256)
                if not first:
                    value = value + ref[where]
                ref[where] = value
            else:
                cols = pl.ds(pl.multiple_of(i * 128, 128), 128)
                value = jnp.concatenate(
                    [mm_first(H[0, rows, cols], X[1, half, rows]) for half in range(2)], axis=1
                )
                if not first:
                    value = value + down_w[cols]
                down_w[cols] = value
            return jnp.maximum(top, largest(value)) if last else top

        top = lax.fori_loop(0, 4 if kind < 2 else 7, tile, jnp.zeros((8, 128), F32))
        if last:
            set_top(kind // 2, kind % 2, top)

    pulls = Batch(IGS)
    pull_sems = [new("recv") for _ in range(2)]
    across = Batch(CS.at[pl.ds(0, 12)])
    across_sems = [new("recv") for _ in range(3)]

    def input_part(start, count, batch):
        rows = pl.ds(start, count)

        def half_value(half):
            return scales[0] * mm_last(H[1, rows], W[0, half]) + scales[1] * mm_last(H[2, rows], W[1, half])

        IGS[rows] = half_value(1 - core).astype(BF16)
        pulls.send(IGS.at[rows], CR.at[rows], partner, pull_sems[batch])
        IGK[rows] = half_value(core)

    def input_across(lower, upper):
        def block(r, carry):
            q = r // 2
            odd = lax.rem(q, 2)
            rel = odd * ((7 - q) // 2) + (1 - odd) * (4 + q // 2)
            c = lax.rem(z + rel, 8)
            px = c // 2
            py = 2 * lax.rem(c, 2) + lax.rem(r, 2)
            da = lax.rem(px + core * (py - px) - a + 4, 4)
            db = lax.rem(py + core * (px - py) - b + 4, 4)

            @pl.when(da != 0)
            def _():
                rows = pl.ds(pl.multiple_of(r * BLK, 16), BLK)
                slot = (da - 1) * 4 + db
                CS[slot] = (IGK[rows] + CR[rows].astype(F32)).astype(BF16)
                for k in range(1, 4):
                    @pl.when(da == k)
                    def _():
                        across.send(CS.at[slot], RA.at[slot], dev(k, 0), across_sems[k - 1])

            return carry

        lax.fori_loop(lower, upper, block, 0)

    groups = [
        [partner],
        [(wide, lax.rem(z + k, 8)) for k in range(1, 8)],
        [dev(k, j) for k in range(4) for j in range(4) if k + j > 0],
    ]

    def maxima(which):
        base = 0
        for phase, group in enumerate(groups):
            out = Batch(MR.at[which, pl.ds(0, len(group))])
            sem = new("recv")
            for k, other in enumerate(group):
                out.send(MX.at[which, phase], MR.at[which, base + k], other, sem)
            yield
            arrived(MR.at[which, pl.ds(0, len(group))], sem)
            value = MX[which, phase]
            for k in range(len(group)):
                value = jnp.maximum(value, MR[which, base + k])
            MX[which, phase + 1] = value
            base += len(group)

    def amax(which, k):
        return jnp.max(MX[which, 3, 4 * k : 4 * k + 4]) + eps

    def scaled(src, dst, top):
        inverse = 1.0 / jnp.full((16, 128), top, F32)
        rows, cols = src.shape
        factor = jnp.concatenate([inverse] * (cols // 128), axis=1)

        def tile(i, carry):
            where = pl.ds(pl.multiple_of(i * 16, 16), 16)
            dst[where] = (src[where] * factor).astype(BF16)
            return carry

        lax.fori_loop(0, rows // 16, tile, 0)

    weight_part(2, 480, 288, True, False)
    step(up_all)
    step(gate_all)
    step(up_all)
    input_part(480, 288, 0)
    step(gate_all)
    step(up_all)
    input_part(288, 192, 0)
    weight_part(0, 288, 480, True, False)
    arrived(CR.at[pl.ds(0, 480)], pull_sems[0])
    input_across(6, 16)
    step(gate_all)
    step(up_all)
    input_part(96, 192, 1)
    weight_part(1, 288, 480, True, False)
    step(gate_all)
    step(up_all)
    input_part(0, 96, 1)
    step(hidden_all)
    weight_part(0, 0, 288, False, True)
    arrived(CR.at[pl.ds(0, 288)], pull_sems[1])
    input_across(0, 6)
    weight_part(1, 0, 288, False, True)
    step(hidden_all)
    first_tops = maxima(0)
    step(first_tops)
    weight_part(2, 288, 192, False, False)
    step(first_tops)
    for sem in across_sems:
        arrived(RA.at[pl.ds(0, 4)], sem)
    along = Batch(BS)
    along_sems = [new("recv") for _ in range(3)]
    for db in (2, 1, 3, 0):
        rows = pl.ds(off(0, db), BLK)
        value = IGK[rows] + CR[rows].astype(F32)
        for k in range(3):
            value = value + RA[4 * k + db].astype(F32)
        if db == 0:
            FS[...] = value
        else:
            BS[db - 1] = value.astype(BF16)
            along.send(BS.at[db - 1], RBB.at[db - 1], dev(0, db), along_sems[db - 1])
    step(hidden_all)
    weight_part(2, 0, 288, False, True)
    value = FS[...]
    for k in range(3):
        arrived(RBB.at[0], along_sems[k])
        value = value + RBB[k].astype(F32)
    FIN[0] = value[:24]
    FIN[1] = value[24:]
    set_top(1, 1, largest(value))
    second_tops = maxima(1)
    step(second_tops)
    last = Batch(FX)
    last_sem = new("recv")
    last.send(FIN.at[1 - core], FX, partner, last_sem)
    step(second_tops)
    step(first_tops)
    run(first_tops)
    scaled(gate_w, gate_o, amax(0, 0))
    step(second_tops)
    scaled(up_w, up_o, amax(0, 1))
    arrived(FX, last_sem)
    mine, theirs = FIN[core], FX[...]
    IGO[:, :HALF] = jnp.where(first_core, mine, theirs)
    IGO[:, HALF:] = jnp.where(first_core, theirs, mine)
    run(second_tops)
    scaled(down_w, down_o, amax(1, 0))
    inverse = 1.0 / jnp.full((24, 128), amax(1, 1), F32)
    input_o[...] = (IGO[...] * jnp.concatenate([inverse] * 8, axis=1)).astype(BF16)
    for k in range(4):
        amax_o[k : k + 1] = jnp.full((1, 128), amax(k // 2, k % 2), F32)
    amax_o[4:] = jnp.zeros((4, 128), F32)

    z_left(0)
    assert (used["send"], used["recv"]) == (N_SEND, N_RECV), used
    for total, sends in finals:
        remote(total, total, partner, sends, 0).wait_send()


def per_device(
    saved_codes,
    saved_scale,
    grad_output,
    gate_codes,
    gate_scale,
    up_codes,
    up_scale,
    down_codes,
    down_scale,
):
    smem = pl.BlockSpec(memory_space=pltpu.SMEM)
    vmem = pl.BlockSpec(memory_space=pltpu.VMEM)
    hbm = pl.BlockSpec(memory_space=pl.ANY)
    gate_out, up_out, down_out, input_out, tops = pl.pallas_call(
        kernel,
        out_shape=[
            pltpu.VMEM((FEAT, UNIT), BF16),
            pltpu.VMEM((FEAT, UNIT), BF16),
            pltpu.VMEM((UNIT, FEAT), BF16),
            pltpu.VMEM((24, FEAT), BF16),
            pltpu.VMEM((8, 128), F32),
        ],
        in_specs=[smem] * 4 + [vmem] * 2 + [hbm] * 3,
        out_specs=[vmem] * 5,
        scratch_shapes=[
            pltpu.VMEM((FEAT, UNIT), F32),
            pltpu.VMEM((FEAT, UNIT), F32),
            pltpu.VMEM((UNIT, FEAT), F32),
            pltpu.VMEM((2, 2, TOK, HALF), BF16),
            pltpu.VMEM((2, 2, HALF, UNIT), BF16),
            pltpu.VMEM((UNIT, FEAT), BF16),
            pltpu.VMEM((2, 2, 24, HALF), F32),
            pltpu.VMEM((2, 24, HALF), F32),
            pltpu.VMEM((3, 672, UNIT), BF16),
            pltpu.VMEM((3, 480, UNIT), BF16),
            pltpu.VMEM((3, 192, UNIT), F32),
            pltpu.VMEM((3, 192, UNIT), F32),
            pltpu.VMEM((3, TOK, UNIT), BF16),
            pltpu.VMEM((3, CH, UNIT), F32),
            pltpu.VMEM((672, UNIT), F32),
            pltpu.VMEM((TOK, HALF), F32),
            pltpu.VMEM((TOK, HALF), BF16),
            pltpu.VMEM((TOK, HALF), BF16),
            pltpu.VMEM((12, BLK, HALF), BF16),
            pltpu.VMEM((12, BLK, HALF), BF16),
            pltpu.VMEM((3, BLK, HALF), BF16),
            pltpu.VMEM((3, BLK, HALF), BF16),
            pltpu.VMEM((BLK, HALF), F32),
            pltpu.VMEM((2, 24, HALF), F32),
            pltpu.VMEM((24, HALF), F32),
            pltpu.VMEM((24, FEAT), F32),
            pltpu.VMEM((2, 4, 8, 128), F32),
            pltpu.VMEM((2, 23, 8, 128), F32),
            pltpu.SemaphoreType.DMA((N_SEND,)),
            pltpu.SemaphoreType.DMA((N_RECV,)),
            pltpu.SemaphoreType.DMA((5,)),
        ],
        compiler_params=pltpu.CompilerParams(
            collective_id=0, has_side_effects=True, vmem_limit_bytes=54 * 1024 * 1024
        ),
    )(
        saved_scale,
        gate_scale,
        up_scale,
        down_scale,
        saved_codes,
        grad_output,
        gate_codes,
        up_codes,
        down_codes,
    )
    return (gate_out, up_out, down_out, input_out, tops[:4, 0])


def solution(mesh):
    placed = (
        P("wide", "narrow"),
        P("wide", "narrow"),
        P("wide", "narrow"),
        P("narrow", "wide"),
        P("narrow", "wide"),
        P("narrow", "wide"),
        P("narrow", "wide"),
        P("wide", "narrow"),
        P("wide", "narrow"),
    )
    return jax.shard_map(
        per_device,
        mesh=mesh,
        in_specs=placed,
        out_specs=(
            P("narrow", "wide"),
            P("narrow", "wide"),
            P("wide", "narrow"),
            P("wide", "narrow"),
            P(),
        ),
        check_vma=False,
    )
```
